512 devices in a mesh: bank: 128 (over y, z, x_hi), tm: 4 (over x_lo, core).
Axes of the slice: x: 4 (x_hi: 2, x_lo: 2; x = x_hi * 2 + x_lo), y: 8, z: 8, core: 2. Of those that a mesh axis runs over, the one named last changes fastest.
Arguments:
- strain: float32 [3, 4, 16384], P(None, 'tm', 'bank'), may hold values from -6 to 6
- fir_taps: float32 [4096], replicated, may hold values from -0.09375 to 0.09375
- templates: bfloat16 [256, 2, 2048], P('bank'), may hold values from -6 to 6
Outputs:
- snr_sq: float32 [3, 256, 65536], P(None, 'bank', 'tm')
- loudest: float32 [3, 65536], P(None, 'tm')
The draws below stay inside these ranges and needn't reach their ends.
All inputs are finite; a program needn't handle non-finite values.
Results may differ from the reference program's by a relative error of at most 0.003.
Values may be sent and summed in bfloat16 or wider, within the bound.
A program may use at most 64 MiB of HBM per device.

```python
import jax
import jax.numpy as jnp
from jax import lax

DET = 3
TLEN = 2048
TAPS = 4096
STRETCH = 16384
STRETCHES = 4
TEMPLATES = 256
N_BANK = 128


def block_levels(stream_key, shape, split, low, high):
    factor_of = 1.0
    for axis_at, blocks in split:
        heights = jax.random.uniform(jax.random.fold_in(jax.random.fold_in(stream_key, 6), axis_at), (blocks,), jnp.float32, low / len(split), high / len(split))
        factor_of = factor_of * jnp.repeat(jnp.exp(heights), shape[axis_at] // blocks).reshape((-1,) + (1,) * (len(shape) - 1 - axis_at))
    return factor_of


def noise(stream_key, shape, width, reach, split=(), held_as=jnp.bfloat16):
    entries = jax.random.normal(stream_key, shape, jnp.float32) * width
    if len(split) > 0:
        entries = block_levels(stream_key, shape, split, -0.22, 0.18) * entries
    return jnp.clip(entries, min=-reach, max=reach).astype(held_as)


def setup_inputs(seed: int = 0) -> dict:
    splits = jax.random.split(jax.random.key(seed), 4)
    strain = noise(splits[0], (DET, STRETCHES, STRETCH), 1.0, 6.0, ((1, 4), (2, 128)), jnp.float32)
    fir_taps = noise(splits[1], (TAPS,), TAPS ** -0.5, 0.09375, (), jnp.float32)
    templates = noise(splits[2], (TEMPLATES, 2, TLEN), 1.0, 6.0, ((0, 128),))
    return dict(strain=strain, fir_taps=fir_taps, templates=templates)


def filter_rows(signal, kernel):
    return lax.conv_general_dilated(signal[:, None, :], kernel, (1,), "VALID", dimension_numbers=("NCH", "OIH", "NCH"), precision=lax.Precision.HIGHEST)


def reference(strain, fir_taps, templates):
    detectors = strain.shape[0]
    series = strain.reshape(detectors, -1)
    total = series.shape[1]
    tap_count = fir_taps.shape[0]
    half_taps = tap_count // 2
    padded = jnp.concatenate([series[:, total - half_taps:], series, series[:, :half_taps - 1]], axis=1)
    whitened = filter_rows(padded, fir_taps.reshape(1, 1, tap_count))[:, 0, :]
    whitened = lax.optimization_barrier(whitened.astype(jnp.bfloat16)).astype(jnp.float32)
    tmpl_len = templates.shape[2]
    lead = tmpl_len // 2
    extended = jnp.concatenate([whitened[:, total - lead:], whitened, whitened[:, :lead - 1]], axis=1)
    wide_tmpl = templates.astype(jnp.float32)
    energy = jnp.mean(jnp.square(wide_tmpl), axis=(1, 2)) + 1e-6
    count = templates.shape[0]
    groups = N_BANK // 8
    per_group = count // groups
    kernels = wide_tmpl.reshape(groups, per_group * 2, 1, tmpl_len)
    divisors = (tmpl_len * energy).reshape(groups, per_group)

    def one_group(pair):
        kernel, divisor = pair
        result = filter_rows(extended, kernel).reshape(detectors, per_group, 2, total)
        return jnp.sum(result * result, axis=2) / divisor[None, :, None]

    stacked = lax.map(one_group, (kernels, divisors))
    snr_sq = jnp.transpose(stacked, (1, 0, 2, 3)).reshape(detectors, count, total)
    return snr_sq, jnp.max(snr_sq, axis=1)
```

```python
import jax
import jax.numpy as jnp
from jax import lax
from jax.experimental import pallas as pl
from jax.experimental.pallas import tpu as pltpu
from jax.sharding import PartitionSpec as P

MESH = pl.DeviceIdType.MESH
LANES = 128
DET = 3
NY, NZ, NX, NT = 8, 8, 2, 4
BANK = NY * NZ * NX
TAPS = 4096
TLEN = 2048
WSTEP = 5
WOFF = 17
CSTEP = 8
COFF = 17


def far_first(i):
    half = (i + 1) // 2
    odd = i % 2
    return 4 + half - 2 * half * odd


def kernel(
    strain, taps, tmpl, snr, loud,
    gath, tap_v, tmpl_v, wtab, ctab, xh, xl, white, cwin, sbuf, rbuf, res,
    in_sem, send_sem, recv_sem, halo_sem,
):
    b = lax.axis_index("bank")
    m = lax.axis_index("tm")
    y, z, x = b // 16, (b // 2) % 8, b % 2
    up, down = (m + 1) % NT, (m + NT - 1) % NT
    pairs = gath.reshape(96, 2, 8, LANES)

    def bank_of(yy, zz, xx):
        return yy * 16 + zz * 2 + xx

    barrier = pltpu.get_barrier_semaphore()

    def greet(dev):
        pl.semaphore_signal(barrier, inc=1, device_id=dev, device_id_type=MESH)

    for j in range(1, NZ):
        greet((bank_of(y, (z + j) % NZ, x), m))
    for j in range(1, NY * NX):
        jy, jx = far_first((j - 1) // 2), j % 2
        greet((bank_of((y + jy) % NY, z, (x + jx) % NX), m))
    for yy in (0, 1):
        for xx in range(NX):
            greet((bank_of(yy, z, xx), up))
    for yy in (6, 7):
        for xx in range(NX):
            greet((bank_of(yy, z, xx), down))

    own_row = pairs.at[12 + 8 * y + z, x, pl.ds(0, DET), :]
    load_own = pltpu.make_async_copy(strain.at[:, 0, :], own_row, in_sem.at[0])
    load_taps = pltpu.make_async_copy(taps, tap_v, in_sem.at[1])
    load_tmpl = pltpu.make_async_copy(tmpl, tmpl_v, in_sem.at[2])
    load_own.start()
    load_taps.start()
    load_tmpl.start()
    load_own.wait()
    load_taps.wait()
    load_tmpl.wait()

    row_id = lax.broadcasted_iota(jnp.int32, (LANES, LANES), 0)
    lane_id = lax.broadcasted_iota(jnp.int32, (LANES, LANES), 1)
    keep = lane_id >= row_id
    zero = jnp.zeros((LANES, LANES), jnp.float32)
    zero_b = jnp.zeros((LANES, LANES), jnp.bfloat16)

    def skew(row):
        wide = jnp.broadcast_to(row, (LANES, LANES))
        return pltpu.roll(wide, 0, 1, stride=1, stride_axis=0)

    def tap_table():
        last = zero
        for c in range(TAPS // LANES + 1):
            if c < TAPS // LANES:
                now = skew(tap_v[pl.ds(c, 1), :])
            else:
                now = zero
            tile = jnp.where(keep, now, last)
            last = now
            hi = tile.astype(jnp.bfloat16)
            lo = (tile - hi.astype(jnp.float32)).astype(jnp.bfloat16)
            for part, val in enumerate((hi, lo)):
                wtab[part, 0:128, c * 128:(c + 1) * 128] = val
                wtab[part, 128:256, (c + 1) * 128:(c + 2) * 128] = val
        for part in range(2):
            wtab[part, 0:128, 33 * 128:34 * 128] = zero_b
            wtab[part, 128:256, 0:128] = zero_b

    def tmpl_table(f):
        last = zero
        rows = tmpl_v[f // 2].astype(jnp.float32)
        for c in range(TLEN // LANES + 1):
            if c < TLEN // LANES:
                now = skew(rows[f % 2:f % 2 + 1, c * 128:(c + 1) * 128])
            else:
                now = zero
            ctab[f * 128:(f + 1) * 128, c * 128:(c + 1) * 128] = jnp.where(keep, now, last).astype(jnp.bfloat16)
            last = now

    edge = jnp.where((y <= 1) | (y >= 6), NY * NX, 0)
    pl.semaphore_wait(barrier, (NZ - 1) + (NY * NX - 1) + edge)

    for j in (4, 3, 5, 2, 6, 1, 7):
        pltpu.make_async_remote_copy(
            src_ref=own_row, dst_ref=own_row, send_sem=send_sem.at[0], recv_sem=recv_sem.at[0],
            device_id=(bank_of(y, (z + j) % NZ, x), m), device_id_type=MESH,
        ).start()
    tap_table()
    got = pairs.at[pl.ds(0, NZ - 1), 0, pl.ds(0, DET), :]
    pltpu.make_async_copy(got, got, recv_sem.at[0]).wait()

    group = pairs.at[pl.ds(12 + 8 * y, 8), x, pl.ds(0, DET), :]
    for i in range(NY * NX - 1):
        jy, jx = far_first(i // 2), 1 - i % 2
        pltpu.make_async_remote_copy(
            src_ref=group, dst_ref=group, send_sem=send_sem.at[1], recv_sem=recv_sem.at[1],
            device_id=(bank_of((y + jy) % NY, z, (x + jx) % NX), m), device_id_type=MESH,
        ).start()

    def margin(cond, src_at, dst_at, count, to):
        @pl.when(cond)
        def _():
            for i in range(NY * NX):
                jy, jx = far_first(i // 2), 1 - i % 2
                pltpu.make_async_remote_copy(
                    src_ref=pairs.at[pl.ds(src_at, count), x, pl.ds(0, DET), :],
                    dst_ref=pairs.at[pl.ds(dst_at, count), x, pl.ds(0, DET), :],
                    send_sem=halo_sem.at[0], recv_sem=recv_sem.at[1],
                    device_id=(bank_of((y + jy) % NY, z, (x + jx) % NX), to), device_id_type=MESH,
                ).start()

    margin(y == 0, 12, 76, 8, down)
    margin(y == 1, 20, 84, 4, down)
    margin(y == 6, 64, 0, 4, up)
    margin(y == 7, 68, 4, 8, up)

    for f in range(4):
        tmpl_table(f)
    inv = []
    for k in range(2):
        wide = tmpl_v[k].astype(jnp.float32)
        energy = jnp.sum(wide * wide, keepdims=True) / (2.0 * TLEN) + 1e-6
        inv.append(1.0 / (TLEN * energy))

    got = pairs.at[pl.ds(0, 84), :, pl.ds(0, DET), :]
    pltpu.make_async_copy(got, got, recv_sem.at[1]).wait()

    for d in range(DET):
        for a in range(WSTEP + WOFF - 1):
            for h in range(2):
                val = gath[pl.ds(8 * (2 * a + h) + d, 16, stride=16 * WSTEP), :]
                hi = val.astype(jnp.bfloat16)
                lo = (val - hi.astype(jnp.float32)).astype(jnp.bfloat16)
                for o in range(WOFF):
                    if 0 <= a - o < WSTEP:
                        lanes = slice(o * 256 + h * 128, o * 256 + h * 128 + 128)
                        xh[(a - o) * 16:(a - o + 1) * 16, lanes] = hi
                        xl[(a - o) * 16:(a - o + 1) * 16, lanes] = lo
        nt = (((1,), (1,)), ((), ()))
        hi_all = xh[...]
        out = lax.dot_general(hi_all, wtab[0], nt, preferred_element_type=jnp.float32)
        out += lax.dot_general(hi_all, wtab[1], nt, preferred_element_type=jnp.float32)
        out += lax.dot_general(xl[...], wtab[0], nt, preferred_element_type=jnp.float32)
        for a in range(WSTEP):
            for h in range(2):
                white[pl.ds(2 * a + h, 16, stride=2 * WSTEP), :] = out[a * 16:(a + 1) * 16, h * 128:(h + 1) * 128]
        for a in range(CSTEP + COFF - 1):
            val = white[pl.ds(a, 16, stride=CSTEP), :].astype(jnp.bfloat16)
            for o in range(COFF):
                if 0 <= a - o < CSTEP:
                    cwin[(a - o) * 16:(a - o + 1) * 16, o * 128:(o + 1) * 128] = val
        corr = lax.dot_general(cwin[...], ctab[...], nt, preferred_element_type=jnp.float32)
        power = []
        for k in range(2):
            c0 = corr[:, k * 256:k * 256 + 128]
            c1 = corr[:, k * 256 + 128:k * 256 + 256]
            power.append((c0 * c0 + c1 * c1) * inv[k])
        best = jnp.maximum(power[0], power[1])
        for a in range(CSTEP):
            rows = slice(a * 16, (a + 1) * 16)
            for k in range(2):
                snr[pl.ds(d * 256 + 2 * a + k, 16, stride=16), :] = power[k][rows]
            sbuf[pl.ds(8 * a + d, 16, stride=64), :] = best[rows]

    send3 = sbuf.reshape(BANK, 8, LANES)

    def scatter(i, carry):
        jx = 1 - i // 64
        jy, jz = far_first((i // 8) % 8), far_first(i % 8)
        p = bank_of((y + jy) % NY, (z + jz) % NZ, (x + jx) % NX)
        pltpu.make_async_remote_copy(
            src_ref=send3.at[p, pl.ds(0, DET), :], dst_ref=rbuf.at[b, pl.ds(0, DET), :],
            send_sem=send_sem.at[2], recv_sem=recv_sem.at[2],
            device_id=(p, m), device_id_type=MESH,
        ).start()
        return carry

    lax.fori_loop(0, BANK - 1, scatter, 0)
    own = send3[b, 0:DET, :]
    got = rbuf.at[pl.ds(0, BANK - 1), pl.ds(0, DET), :]
    pltpu.make_async_copy(got, got, recv_sem.at[2]).wait()
    rbuf[b, 0:DET, :] = own
    top = jnp.max(rbuf[:, 0:DET, :], axis=0)
    res[...] = top
    mine = pl.ds(pl.multiple_of(b * 128, 128), 128)

    def spread(i, carry):
        jx = 1 - i // 64
        jy, jz = far_first((i // 8) % 8), far_first(i % 8)
        p = bank_of((y + jy) % NY, (z + jz) % NZ, (x + jx) % NX)
        pltpu.make_async_remote_copy(
            src_ref=res, dst_ref=loud.at[:, mine],
            send_sem=send_sem.at[3], recv_sem=recv_sem.at[3],
            device_id=(p, m), device_id_type=MESH,
        ).start()
        return carry

    lax.fori_loop(0, BANK - 1, spread, 0)
    loud[:, mine] = top
    got = rbuf.at[pl.ds(0, BANK - 1), pl.ds(0, DET), :]
    pltpu.make_async_copy(got, got, recv_sem.at[3]).wait()
    sent = pairs.at[pl.ds(0, NZ - 1), 0, pl.ds(0, DET), :]
    pltpu.make_async_copy(sent, sent, send_sem.at[0]).wait()
    sent = pairs.at[pl.ds(0, 60), :, pl.ds(0, DET), :]
    pltpu.make_async_copy(sent, sent, send_sem.at[1]).wait()

    @pl.when((y == 0) | (y == 7))
    def _():
        part = pairs.at[pl.ds(0, 64), :, pl.ds(0, DET), :]
        pltpu.make_async_copy(part, part, halo_sem.at[0]).wait()

    @pl.when((y == 1) | (y == 6))
    def _():
        part = pairs.at[pl.ds(0, 32), :, pl.ds(0, DET), :]
        pltpu.make_async_copy(part, part, halo_sem.at[0]).wait()

    sent = rbuf.at[pl.ds(0, BANK - 1), pl.ds(0, DET), :]
    pltpu.make_async_copy(sent, sent, send_sem.at[2]).wait()
    pltpu.make_async_copy(sent, sent, send_sem.at[3]).wait()


def shards(strain, fir_taps, templates):
    any_spec = pl.BlockSpec(memory_space=pl.ANY)
    vmem_spec = pl.BlockSpec(memory_space=pltpu.VMEM)
    snr, loud = pl.pallas_call(
        kernel,
        out_shape=(
            jax.ShapeDtypeStruct((DET * 256, LANES), jnp.float32),
            jax.ShapeDtypeStruct((DET, BANK * LANES), jnp.float32),
        ),
        in_specs=[any_spec, any_spec, any_spec],
        out_specs=(vmem_spec, vmem_spec),
        scratch_shapes=[
            pltpu.VMEM((96 * 16, LANES), jnp.float32),
            pltpu.VMEM((TAPS // LANES, LANES), jnp.float32),
            pltpu.VMEM((2, 2, TLEN), jnp.bfloat16),
            pltpu.VMEM((2, 256, WOFF * 256), jnp.bfloat16),
            pltpu.VMEM((512, COFF * 128), jnp.bfloat16),
            pltpu.VMEM((WSTEP * 16, WOFF * 256), jnp.bfloat16),
            pltpu.VMEM((WSTEP * 16, WOFF * 256), jnp.bfloat16),
            pltpu.VMEM((160, LANES), jnp.float32),
            pltpu.VMEM((CSTEP * 16, COFF * 128), jnp.bfloat16),
            pltpu.VMEM((BANK * 8, LANES), jnp.float32),
            pltpu.VMEM((BANK, 8, LANES), jnp.float32),
            pltpu.VMEM((DET, LANES), jnp.float32),
            pltpu.SemaphoreType.DMA((3,)),
            pltpu.SemaphoreType.DMA((4,)),
            pltpu.SemaphoreType.DMA((4,)),
            pltpu.SemaphoreType.DMA((1,)),
        ],
        compiler_params=pltpu.CompilerParams(
            collective_id=0, has_side_effects=True, vmem_limit_bytes=32 * 1024 * 1024
        ),
        name="matched_filter",
    )(strain, fir_taps.reshape(TAPS // LANES, LANES), templates)
    snr = snr.reshape(DET, 128, 2, LANES).transpose(0, 2, 1, 3).reshape(DET, 2, 128 * LANES)
    return snr, loud


def solution(mesh):
    in_specs = (P(None, "tm", "bank"), P(), P("bank", None, None))
    out_specs = (P(None, "bank", "tm"), P(None, "tm"))
    return jax.shard_map(shards, mesh=mesh, in_specs=in_specs, out_specs=out_specs, check_vma=False)
```

```python
import jax
import jax.numpy as jnp
from jax import lax
from jax.experimental import pallas as pl
from jax.experimental.pallas import tpu as pltpu
from jax.sharding import PartitionSpec as P

MESH = pl.DeviceIdType.MESH
LANES = 128
DET = 3
NY, NZ, NX, NT = 8, 8, 2, 4
BANK = NY * NZ * NX
TAPS = 4096
TLEN = 2048
WSTEP = 5
WOFF = 17
CSTEP = 8
COFF = 17
ROWS = 16 * DET


def far_first(i):
    half = (i + 1) // 2
    odd = i % 2
    return 4 + half - 2 * half * odd


def kernel(
    strain, taps, tmpl, snr, loud,
    gath, tap_v, tmpl_v, wtab, ctab, xh, xl, white, cwin, sbuf, rbuf, res,
    in_sem, send_sem, recv_sem, halo_sem,
):
    b = lax.axis_index("bank")
    m = lax.axis_index("tm")
    y, z, x = b // 16, (b // 2) % 8, b % 2
    up, down = (m + 1) % NT, (m + NT - 1) % NT
    pairs = gath.reshape(96, 2, 8, LANES)

    def bank_of(yy, zz, xx):
        return yy * 16 + zz * 2 + xx

    barrier = pltpu.get_barrier_semaphore()

    def greet(dev):
        pl.semaphore_signal(barrier, inc=1, device_id=dev, device_id_type=MESH)

    for j in range(1, 8):
        jj = far_first(j - 1)
        greet((bank_of((y + jj) % NY, z, 1 - x), m))
        greet((bank_of(y, (z + jj) % NZ, 1 - x), m))
        greet((bank_of((y + jj) % NY, z, x), m))
        greet((bank_of(y, (z + jj) % NZ, x), m))
    greet((bank_of(y, z, 1 - x), m))
    for j in range(NZ):
        greet((bank_of(y, j, x), up))
        greet((bank_of(y, j, x), down))
    for yy in (0, 1):
        greet((bank_of(yy, z, x), up))
        greet((bank_of(6 + yy, z, x), down))

    own_row = pairs.at[12 + 8 * y + z, x, pl.ds(0, DET), :]
    load_own = pltpu.make_async_copy(strain.at[:, 0, :], own_row, in_sem.at[0])
    load_taps = pltpu.make_async_copy(taps, tap_v, in_sem.at[1])
    load_tmpl = pltpu.make_async_copy(tmpl, tmpl_v, in_sem.at[2])
    load_own.start()
    load_taps.start()
    load_tmpl.start()
    load_own.wait()
    load_taps.wait()
    load_tmpl.wait()

    row_id = lax.broadcasted_iota(jnp.int32, (LANES, LANES), 0)
    lane_id = lax.broadcasted_iota(jnp.int32, (LANES, LANES), 1)
    keep = lane_id >= row_id
    zero = jnp.zeros((LANES, LANES), jnp.float32)
    zero_b = jnp.zeros((LANES, LANES), jnp.bfloat16)

    def skew(row):
        wide = jnp.broadcast_to(row, (LANES, LANES))
        return pltpu.roll(wide, 0, 1, stride=1, stride_axis=0)

    def tap_table():
        last = zero
        for c in range(TAPS // LANES + 1):
            if c < TAPS // LANES:
                now = skew(tap_v[pl.ds(c, 1), :])
            else:
                now = zero
            tile = jnp.where(keep, now, last)
            last = now
            hi = tile.astype(jnp.bfloat16)
            lo = (tile - hi.astype(jnp.float32)).astype(jnp.bfloat16)
            for part, val in enumerate((hi, lo)):
                wtab[part, 0:128, c * 128:(c + 1) * 128] = val
                wtab[part, 128:256, (c + 1) * 128:(c + 2) * 128] = val
        for part in range(2):
            wtab[part, 0:128, 33 * 128:34 * 128] = zero_b
            wtab[part, 128:256, 0:128] = zero_b

    def tmpl_table(f):
        last = zero
        rows = tmpl_v[f // 2].astype(jnp.float32)
        for c in range(TLEN // LANES + 1):
            if c < TLEN // LANES:
                now = skew(rows[f % 2:f % 2 + 1, c * 128:(c + 1) * 128])
            else:
                now = zero
            ctab[f * 128:(f + 1) * 128, c * 128:(c + 1) * 128] = jnp.where(keep, now, last).astype(jnp.bfloat16)
            last = now

    edge = jnp.where((y <= 1) | (y >= 6), NY, 0)
    pl.semaphore_wait(barrier, 29 + 2 * NZ + edge)

    def send_a(p):
        pltpu.make_async_remote_copy(
            src_ref=own_row, dst_ref=own_row, send_sem=send_sem.at[0], recv_sem=recv_sem.at[0],
            device_id=(p, m), device_id_type=MESH,
        ).start()

    for j in range(15):
        jj, dx = far_first(j // 2), 1 - j % 2
        send_a(jnp.where(
            x == 0, bank_of((y + jj) % NY, z, (x + dx) % NX), bank_of(y, (z + jj) % NZ, (x + dx) % NX)
        ))
    tap_table()
    got = pairs.at[pl.ds(0, 15), 0, pl.ds(0, DET), :]
    pltpu.make_async_copy(got, got, recv_sem.at[0]).wait()

    def send_b(src, dst, sem, p, to):
        pltpu.make_async_remote_copy(
            src_ref=src, dst_ref=dst, send_sem=sem, recv_sem=recv_sem.at[1],
            device_id=(p, to), device_id_type=MESH,
        ).start()

    eights = gath.reshape(12, 8, 2, 8, LANES)
    at_q, at_r = (12 + z) // 8, (z + 4) % 8
    yline = eights.at[pl.ds(at_q, 8), at_r, 0, pl.ds(0, DET), :]
    zline = pairs.at[pl.ds(12 + 8 * y, 8), 1, pl.ds(0, DET), :]
    for j in range(7):
        jj = far_first(j)
        send_b(yline, yline, send_sem.at[1], bank_of(y, (z + jj) % NZ, x), m)
        send_b(zline, zline, send_sem.at[1], bank_of((y + jj) % NY, z, x), m)

    def margin_y(cond, src_at, dst_at, count, to):
        @pl.when(cond)
        def _():
            for j in range(NY):
                send_b(
                    pairs.at[pl.ds(src_at, count), 1, pl.ds(0, DET), :],
                    pairs.at[pl.ds(dst_at, count), 1, pl.ds(0, DET), :],
                    halo_sem.at[0], bank_of((y + far_first(j)) % NY, z, x), to,
                )

    margin_y(y == 0, 12, 76, 8, down)
    margin_y(y == 1, 20, 84, 4, down)
    margin_y(y == 6, 64, 0, 4, up)
    margin_y(y == 7, 68, 4, 8, up)

    def margin_z(cond, low, high):
        @pl.when(cond)
        def _():
            for j in range(NZ):
                p = bank_of(y, (z + far_first(j)) % NZ, x)
                send_b(
                    eights.at[pl.ds(at_q, low), at_r, 0, pl.ds(0, DET), :],
                    eights.at[pl.ds(at_q + 8, low), at_r, 0, pl.ds(0, DET), :],
                    halo_sem.at[1], p, down,
                )
                send_b(
                    eights.at[pl.ds(8, high), at_r, 0, pl.ds(0, DET), :],
                    eights.at[pl.ds(0, high), at_r, 0, pl.ds(0, DET), :],
                    halo_sem.at[1], p, up,
                )

    margin_z(z < 4, 2, 1)
    margin_z(z >= 4, 1, 2)

    for f in range(4):
        tmpl_table(f)
    inv = []
    for k in range(2):
        wide = tmpl_v[k].astype(jnp.float32)
        energy = jnp.sum(wide * wide, keepdims=True) / (2.0 * TLEN) + 1e-6
        inv.append(1.0 / (TLEN * energy))

    got = pairs.at[pl.ds(0, 80), :, pl.ds(0, DET), :]
    pltpu.make_async_copy(got, got, recv_sem.at[1]).wait()

    nt = (((1,), (1,)), ((), ()))
    for a in range(WSTEP + WOFF - 1):
        for d in range(DET):
            rows = slice(a * ROWS + d * 16, a * ROWS + d * 16 + 16)
            for h in range(2):
                val = gath[pl.ds(8 * (2 * a + h) + d, 16, stride=16 * WSTEP), :]
                hi = val.astype(jnp.bfloat16)
                lo = (val - hi.astype(jnp.float32)).astype(jnp.bfloat16)
                xh[rows, h * 128:(h + 1) * 128] = hi
                xl[rows, h * 128:(h + 1) * 128] = lo
    hi_all = jnp.concatenate([xh[o * ROWS:(o + WSTEP) * ROWS, :] for o in range(WOFF)], axis=1)
    lo_all = jnp.concatenate([xl[o * ROWS:(o + WSTEP) * ROWS, :] for o in range(WOFF)], axis=1)
    both = lax.dot_general(
        jnp.concatenate([hi_all, lo_all], axis=0), wtab[0], nt, preferred_element_type=jnp.float32
    )
    out = both[:WSTEP * ROWS] + both[WSTEP * ROWS:]
    out += lax.dot_general(hi_all, wtab[1], nt, preferred_element_type=jnp.float32)
    for a in range(WSTEP):
        for d in range(DET):
            rows = slice(a * ROWS + d * 16, a * ROWS + d * 16 + 16)
            for h in range(2):
                white[pl.ds(d * 160 + 2 * a + h, 16, stride=2 * WSTEP), :] = out[rows, h * 128:(h + 1) * 128]

    for a in range(CSTEP + COFF - 1):
        for d in range(DET):
            rows = slice(a * ROWS + d * 16, a * ROWS + d * 16 + 16)
            cwin[rows, :] = white[pl.ds(d * 160 + a, 16, stride=CSTEP), :].astype(jnp.bfloat16)
    wins = jnp.concatenate([cwin[o * ROWS:(o + CSTEP) * ROWS, :] for o in range(COFF)], axis=1)
    corr = lax.dot_general(wins, ctab[...], nt, preferred_element_type=jnp.float32)
    power = []
    for k in range(2):
        c0 = corr[:, k * 256:k * 256 + 128]
        c1 = corr[:, k * 256 + 128:k * 256 + 256]
        power.append((c0 * c0 + c1 * c1) * inv[k])
    best = jnp.maximum(power[0], power[1])
    for a in range(CSTEP):
        for d in range(DET):
            rows = slice(a * ROWS + d * 16, a * ROWS + d * 16 + 16)
            for k in range(2):
                snr[pl.ds(d * 256 + 2 * a + k, 16, stride=16), :] = power[k][rows]
            sbuf[pl.ds(8 * a + d, 16, stride=64), :] = best[rows]

    send3 = sbuf.reshape(BANK, 8, LANES)

    far = (4, 3, 5, 2, 6, 1, 7, 0)
    zs = [((z + jz) % NZ) * 2 for jz in far]

    def to_all(make):
        def some(i, carry):
            jx, jy = 1 - i // 8, far_first(i % 8)
            base = bank_of((y + jy) % NY, 0, (x + jx) % NX)
            for n in range(8):
                make(base + zs[n]).start()
            return carry

        lax.fori_loop(0, 15, some, 0)
        base = bank_of(y, 0, x)
        for n in range(7):
            make(base + zs[n]).start()

    to_all(lambda p: pltpu.make_async_remote_copy(
        src_ref=send3.at[p, pl.ds(0, DET), :], dst_ref=rbuf.at[b, pl.ds(0, DET), :],
        send_sem=send_sem.at[2], recv_sem=recv_sem.at[2],
        device_id=(p, m), device_id_type=MESH,
    ))
    own = send3[b, 0:DET, :]
    got = rbuf.at[pl.ds(0, BANK - 1), pl.ds(0, DET), :]
    pltpu.make_async_copy(got, got, recv_sem.at[2]).wait()
    rbuf[b, 0:DET, :] = own
    top = jnp.max(rbuf[:, 0:DET, :], axis=0)
    res[...] = top
    mine = pl.ds(pl.multiple_of(b * 128, 128), 128)

    to_all(lambda p: pltpu.make_async_remote_copy(
        src_ref=res, dst_ref=loud.at[:, mine],
        send_sem=send_sem.at[3], recv_sem=recv_sem.at[3],
        device_id=(p, m), device_id_type=MESH,
    ))
    loud[:, mine] = top
    got = rbuf.at[pl.ds(0, BANK - 1), pl.ds(0, DET), :]
    pltpu.make_async_copy(got, got, recv_sem.at[3]).wait()
    sent = pairs.at[pl.ds(0, 15), 0, pl.ds(0, DET), :]
    pltpu.make_async_copy(sent, sent, send_sem.at[0]).wait()
    sent = pairs.at[pl.ds(0, 56), :, pl.ds(0, DET), :]
    pltpu.make_async_copy(sent, sent, send_sem.at[1]).wait()
    part = pairs.at[pl.ds(0, 12), :, pl.ds(0, DET), :]
    pltpu.make_async_copy(part, part, halo_sem.at[1]).wait()

    @pl.when((y == 0) | (y == 7))
    def _():
        part = pairs.at[pl.ds(0, 32), :, pl.ds(0, DET), :]
        pltpu.make_async_copy(part, part, halo_sem.at[0]).wait()

    @pl.when((y == 1) | (y == 6))
    def _():
        part = pairs.at[pl.ds(0, 16), :, pl.ds(0, DET), :]
        pltpu.make_async_copy(part, part, halo_sem.at[0]).wait()

    sent = rbuf.at[pl.ds(0, BANK - 1), pl.ds(0, DET), :]
    pltpu.make_async_copy(sent, sent, send_sem.at[2]).wait()
    pltpu.make_async_copy(sent, sent, send_sem.at[3]).wait()


def shards(strain, fir_taps, templates):
    any_spec = pl.BlockSpec(memory_space=pltpu.HBM)
    vmem_spec = pl.BlockSpec(memory_space=pltpu.VMEM)
    snr, loud = pl.pallas_call(
        kernel,
        out_shape=(
            jax.ShapeDtypeStruct((DET * 256, LANES), jnp.float32),
            jax.ShapeDtypeStruct((DET, BANK * LANES), jnp.float32),
        ),
        in_specs=[any_spec, any_spec, any_spec],
        out_specs=(vmem_spec, vmem_spec),
        scratch_shapes=[
            pltpu.VMEM((96 * 16, LANES), jnp.float32),
            pltpu.VMEM((TAPS // LANES, LANES), jnp.float32),
            pltpu.VMEM((2, 2, TLEN), jnp.bfloat16),
            pltpu.VMEM((2, 256, WOFF * 256), jnp.bfloat16),
            pltpu.VMEM((512, COFF * 128), jnp.bfloat16),
            pltpu.VMEM(((WSTEP + WOFF - 1) * ROWS, 256), jnp.bfloat16),
            pltpu.VMEM(((WSTEP + WOFF - 1) * ROWS, 256), jnp.bfloat16),
            pltpu.VMEM((DET * 160, LANES), jnp.float32),
            pltpu.VMEM(((CSTEP + COFF - 1) * ROWS, LANES), jnp.bfloat16),
            pltpu.VMEM((BANK * 8, LANES), jnp.float32),
            pltpu.VMEM((BANK, 8, LANES), jnp.float32),
            pltpu.VMEM((DET, LANES), jnp.float32),
            pltpu.SemaphoreType.DMA((3,)),
            pltpu.SemaphoreType.DMA((4,)),
            pltpu.SemaphoreType.DMA((4,)),
            pltpu.SemaphoreType.DMA((2,)),
        ],
        compiler_params=pltpu.CompilerParams(
            collective_id=0, has_side_effects=True, vmem_limit_bytes=32 * 1024 * 1024
        ),
        name="matched_filter",
    )(*[pltpu.with_memory_space_constraint(v, pltpu.HBM) for v in (strain, fir_taps.reshape(TAPS // LANES, LANES), templates)])
    snr = snr.reshape(DET, 128, 2, LANES).transpose(0, 2, 1, 3).reshape(DET, 2, 128 * LANES)
    return snr, loud


def solution(mesh):
    in_specs = (P(None, "tm", "bank"), P(), P("bank", None, None))
    out_specs = (P(None, "bank", "tm"), P(None, "tm"))
    return jax.shard_map(shards, mesh=mesh, in_specs=in_specs, out_specs=out_specs, check_vma=False)
```

```python
import jax
import jax.numpy as jnp
from jax import lax
from jax.experimental import pallas as pl
from jax.experimental.pallas import tpu as pltpu
from jax.sharding import PartitionSpec as P

MESH = pl.DeviceIdType.MESH
LANES = 128
DET = 3
NY, NZ, NX, NT = 8, 8, 2, 4
BANK = NY * NZ * NX
TAPS = 4096
TLEN = 2048
WSTEP = 5
WOFF = 17
COFF = 9
ROWS = 16 * DET


def far_first(i):
    half = (i + 1) // 2
    odd = i % 2
    return 4 + half - 2 * half * odd


def kernel(
    strain, taps, tmpl, snr, loud,
    gath, tap_v, tmpl_v, wtab, ctab, xh, xl, acc, cwin, sbuf, rbuf, res,
    in_sem, send_sem, recv_sem, halo_sem,
):
    b = lax.axis_index("bank")
    m = lax.axis_index("tm")
    y, z, x = b // 16, (b // 2) % 8, b % 2
    up, down = (m + 1) % NT, (m + NT - 1) % NT
    pairs = gath.reshape(96, 2, 8, LANES)

    def bank_of(yy, zz, xx):
        return yy * 16 + zz * 2 + xx

    barrier = pltpu.get_barrier_semaphore()

    def greet(dev):
        pl.semaphore_signal(barrier, inc=1, device_id=dev, device_id_type=MESH)

    for j in range(1, 8):
        jj = far_first(j - 1)
        greet((bank_of((y + jj) % NY, z, 1 - x), m))
        greet((bank_of(y, (z + jj) % NZ, 1 - x), m))
        greet((bank_of((y + jj) % NY, z, x), m))
        greet((bank_of(y, (z + jj) % NZ, x), m))
    greet((bank_of(y, z, 1 - x), m))
    for j in range(NZ):
        greet((bank_of(y, j, x), up))
        greet((bank_of(y, j, x), down))
    for yy in (0, 1):
        greet((bank_of(yy, z, x), up))
        greet((bank_of(6 + yy, z, x), down))

    own_row = pairs.at[12 + 8 * y + z, x, pl.ds(0, DET), :]
    load_own = pltpu.make_async_copy(strain.at[:, 0, :], own_row, in_sem.at[0])
    load_taps = pltpu.make_async_copy(taps, tap_v, in_sem.at[1])
    load_tmpl = pltpu.make_async_copy(tmpl, tmpl_v, in_sem.at[2])
    load_own.start()
    load_taps.start()
    load_tmpl.start()
    load_own.wait()
    load_taps.wait()
    load_tmpl.wait()

    row_id = lax.broadcasted_iota(jnp.int32, (LANES, LANES), 0)
    lane_id = lax.broadcasted_iota(jnp.int32, (LANES, LANES), 1)
    keep = lane_id >= row_id
    zero = jnp.zeros((LANES, LANES), jnp.float32)
    zero_b = jnp.zeros((LANES, LANES), jnp.bfloat16)

    def skew(row):
        wide = jnp.broadcast_to(row, (LANES, LANES))
        return pltpu.roll(wide, 0, 1, stride=1, stride_axis=0)

    def tap_table():
        last = zero
        for c in range(TAPS // LANES + 1):
            if c < TAPS // LANES:
                now = skew(tap_v[pl.ds(c, 1), :])
            else:
                now = zero
            tile = jnp.where(keep, now, last)
            last = now
            hi = tile.astype(jnp.bfloat16)
            lo = (tile - hi.astype(jnp.float32)).astype(jnp.bfloat16)
            for part, val in enumerate((hi, lo)):
                wtab[part, 0:128, c * 128:(c + 1) * 128] = val
                wtab[part, 128:256, (c + 1) * 128:(c + 2) * 128] = val
        for part in range(2):
            wtab[part, 0:128, 33 * 128:34 * 128] = zero_b
            wtab[part, 128:256, 0:128] = zero_b

    def tmpl_table(f):
        last = zero
        rows = tmpl_v[f // 2].astype(jnp.float32)
        top, low = slice(f * 256, f * 256 + 128), slice(f * 256 + 128, f * 256 + 256)
        for c in range(TLEN // LANES + 1):
            if c < TLEN // LANES:
                now = skew(rows[f % 2:f % 2 + 1, c * 128:(c + 1) * 128])
            else:
                now = zero
            tile = jnp.where(keep, now, last).astype(jnp.bfloat16)
            last = now
            ctab[top, c * 128:(c + 1) * 128] = tile
            ctab[low, (c + 1) * 128:(c + 2) * 128] = tile
        ctab[top, 17 * 128:18 * 128] = zero_b
        ctab[low, 0:128] = zero_b

    tap_table()
    tmpl_table(0)
    tmpl_table(1)
    edge = jnp.where((y <= 1) | (y >= 6), NY, 0)
    pl.semaphore_wait(barrier, 29 + 2 * NZ + edge)

    def send_a(p):
        pltpu.make_async_remote_copy(
            src_ref=own_row, dst_ref=own_row, send_sem=send_sem.at[0], recv_sem=recv_sem.at[0],
            device_id=(p, m), device_id_type=MESH,
        ).start()

    for j in range(15):
        jj, dx = far_first(j // 2), 1 - j % 2
        send_a(jnp.where(
            x == 0, bank_of((y + jj) % NY, z, (x + dx) % NX), bank_of(y, (z + jj) % NZ, (x + dx) % NX)
        ))
    tmpl_table(2)
    tmpl_table(3)
    inv = []
    for k in range(2):
        wide = tmpl_v[k].astype(jnp.float32)
        energy = jnp.sum(wide * wide, keepdims=True) / (2.0 * TLEN) + 1e-6
        inv.append(1.0 / (TLEN * energy))

    got = pairs.at[pl.ds(0, 15), 0, pl.ds(0, DET), :]
    pltpu.make_async_copy(got, got, recv_sem.at[0]).wait()

    def send_b(src, dst, sem, p, to):
        pltpu.make_async_remote_copy(
            src_ref=src, dst_ref=dst, send_sem=sem, recv_sem=recv_sem.at[1],
            device_id=(p, to), device_id_type=MESH,
        ).start()

    eights = gath.reshape(12, 8, 2, 8, LANES)
    at_q, at_r = (12 + z) // 8, (z + 4) % 8
    yline = eights.at[pl.ds(at_q, 8), at_r, 0, pl.ds(0, DET), :]
    zline = pairs.at[pl.ds(12 + 8 * y, 8), 1, pl.ds(0, DET), :]
    for j in range(7):
        jj = far_first(j)
        send_b(yline, yline, send_sem.at[1], bank_of(y, (z + jj) % NZ, x), m)
        send_b(zline, zline, send_sem.at[1], bank_of((y + jj) % NY, z, x), m)

    def margin_y(cond, src_at, dst_at, count, to):
        @pl.when(cond)
        def _():
            for j in range(NY):
                send_b(
                    pairs.at[pl.ds(src_at, count), 1, pl.ds(0, DET), :],
                    pairs.at[pl.ds(dst_at, count), 1, pl.ds(0, DET), :],
                    halo_sem.at[0], bank_of((y + far_first(j)) % NY, z, x), to,
                )

    margin_y(y == 0, 12, 76, 8, down)
    margin_y(y == 1, 20, 84, 4, down)
    margin_y(y == 6, 64, 0, 4, up)
    margin_y(y == 7, 68, 4, 8, up)

    def margin_z(cond, low, high):
        @pl.when(cond)
        def _():
            for j in range(NZ):
                p = bank_of(y, (z + far_first(j)) % NZ, x)
                send_b(
                    eights.at[pl.ds(at_q, low), at_r, 0, pl.ds(0, DET), :],
                    eights.at[pl.ds(at_q + 8, low), at_r, 0, pl.ds(0, DET), :],
                    halo_sem.at[1], p, down,
                )
                send_b(
                    eights.at[pl.ds(8, high), at_r, 0, pl.ds(0, DET), :],
                    eights.at[pl.ds(0, high), at_r, 0, pl.ds(0, DET), :],
                    halo_sem.at[1], p, up,
                )

    margin_z(z < 4, 2, 1)
    margin_z(z >= 4, 1, 2)

    got = pairs.at[pl.ds(0, 80), :, pl.ds(0, DET), :]
    pltpu.make_async_copy(got, got, recv_sem.at[1]).wait()

    nt = (((1,), (1,)), ((), ()))

    @pl.when(b >= 0)
    def _():
        for a in range(WSTEP + WOFF - 1):
            for d in range(DET):
                rows = slice(a * ROWS + d * 16, a * ROWS + d * 16 + 16)
                for h in range(2):
                    val = gath[pl.ds(8 * (2 * a + h) + d, 16, stride=16 * WSTEP), :]
                    hi = val.astype(jnp.bfloat16)
                    lo = (val - hi.astype(jnp.float32)).astype(jnp.bfloat16)
                    xh[rows, h * 128:(h + 1) * 128] = hi
                    xl[rows, h * 128:(h + 1) * 128] = lo
        hi_all = jnp.concatenate([xh[o * ROWS:(o + WSTEP) * ROWS, :] for o in range(WOFF)], axis=1)
        lo_all = jnp.concatenate([xl[o * ROWS:(o + WSTEP) * ROWS, :] for o in range(WOFF)], axis=1)
        both = lax.dot_general(
            jnp.concatenate([hi_all, lo_all], axis=0), wtab[0], nt, preferred_element_type=jnp.float32
        )
        acc[...] = both[:WSTEP * ROWS] + both[WSTEP * ROWS:] + lax.dot_general(
            hi_all, wtab[1], nt, preferred_element_type=jnp.float32
        )

    n_out = WSTEP * ROWS
    out = acc[...]
    n_more = (COFF - 1 - WSTEP) * ROWS
    cwin[0:n_out, :] = out.astype(jnp.bfloat16)
    cwin[n_out:2 * n_out, :] = pltpu.roll(out, n_out - 1, 0).astype(jnp.bfloat16)
    cwin[2 * n_out:2 * n_out + n_more, :] = pltpu.roll(out, n_out - 2, 0)[:n_more].astype(jnp.bfloat16)
    wins = jnp.concatenate([cwin[o * ROWS:o * ROWS + n_out, :] for o in range(COFF)], axis=1)
    corr = lax.dot_general(wins, ctab[...], nt, preferred_element_type=jnp.float32)
    power = []
    for k in range(2):
        c0 = corr[:, k * 512:k * 512 + 256]
        c1 = corr[:, k * 512 + 256:k * 512 + 512]
        power.append((c0 * c0 + c1 * c1) * inv[k])
    best = jnp.maximum(power[0], power[1])
    for a in range(WSTEP):
        for d in range(DET):
            rows = slice(a * ROWS + d * 16, a * ROWS + d * 16 + 16)
            for h in range(2):
                sbuf[pl.ds(8 * (2 * a + h) + d, 16, stride=16 * WSTEP), :] = best[rows, h * 128:(h + 1) * 128]

    send3 = sbuf.reshape(160, 8, LANES)

    ys = [((y + j) % NY) * 16 for j in range(NY)]
    zs = [((z + j) % NZ) * 2 for j in range(NZ)]
    xs = [x, 1 - x]
    steps = sorted(
        ((2 * jx + min(jy, NY - jy) + min(jz, NZ - jz), jx, jy, jz)
         for jx in range(NX) for jy in range(NY) for jz in range(NZ)), reverse=True
    )[:BANK - 1]

    def to_all(make):
        for n, (hops, jx, jy, jz) in enumerate(steps):
            make(ys[jy] + zs[jz] + xs[jx]).start()

    to_all(lambda p: pltpu.make_async_remote_copy(
        src_ref=send3.at[p, pl.ds(0, DET), :], dst_ref=rbuf.at[b, pl.ds(0, DET), :],
        send_sem=send_sem.at[2], recv_sem=recv_sem.at[2],
        device_id=(p, m), device_id_type=MESH,
    ))
    for a in range(WSTEP):
        count = (63 - a) // WSTEP + 1
        for d in range(DET):
            rows = slice(a * ROWS + d * 16, a * ROWS + d * 16 + count)
            for h in range(2):
                for k in range(2):
                    snr[pl.ds(d * 256 + 2 * (2 * a + h) + k, count, stride=4 * WSTEP), :] = (
                        power[k][rows, h * 128:(h + 1) * 128]
                    )
    own = send3[b, 0:DET, :]
    got = rbuf.at[pl.ds(0, BANK - 1), pl.ds(0, DET), :]
    pltpu.make_async_copy(got, got, recv_sem.at[2]).wait()
    rbuf[b, 0:DET, :] = own
    top = jnp.max(rbuf[:, 0:DET, :], axis=0)
    res[...] = top
    mine = pl.ds(pl.multiple_of(b * 128, 128), 128)

    def spread(p):
        return pltpu.make_async_remote_copy(
            src_ref=res, dst_ref=loud.at[:, mine],
            send_sem=send_sem.at[3], recv_sem=recv_sem.at[3],
            device_id=(p, m), device_id_type=MESH,
        )

    planes = sorted(
        ((2 * jx + min(jy, NY - jy), jx, jy) for jx in range(NX) for jy in range(NY)), reverse=True
    )
    for zz in range(NZ):
        for hops, jx, jy in planes:
            copy = spread(ys[jy] + 2 * zz + xs[jx])
            if hops:
                copy.start()
            else:
                pl.when(z != zz)(copy.start)
    loud[:, mine] = top
    got = rbuf.at[pl.ds(0, BANK - 1), pl.ds(0, DET), :]
    pltpu.make_async_copy(got, got, recv_sem.at[3]).wait()
    sent = pairs.at[pl.ds(0, 15), 0, pl.ds(0, DET), :]
    pltpu.make_async_copy(sent, sent, send_sem.at[0]).wait()
    sent = pairs.at[pl.ds(0, 56), :, pl.ds(0, DET), :]
    pltpu.make_async_copy(sent, sent, send_sem.at[1]).wait()
    part = pairs.at[pl.ds(0, 12), :, pl.ds(0, DET), :]
    pltpu.make_async_copy(part, part, halo_sem.at[1]).wait()

    @pl.when((y == 0) | (y == 7))
    def _():
        part = pairs.at[pl.ds(0, 32), :, pl.ds(0, DET), :]
        pltpu.make_async_copy(part, part, halo_sem.at[0]).wait()

    @pl.when((y == 1) | (y == 6))
    def _():
        part = pairs.at[pl.ds(0, 16), :, pl.ds(0, DET), :]
        pltpu.make_async_copy(part, part, halo_sem.at[0]).wait()

    sent = rbuf.at[pl.ds(0, BANK - 1), pl.ds(0, DET), :]
    pltpu.make_async_copy(sent, sent, send_sem.at[2]).wait()
    pltpu.make_async_copy(sent, sent, send_sem.at[3]).wait()


def place(snr_v, loud_v, snr, loud, sem):
    copies = [
        pltpu.make_async_copy(snr_v, snr, sem.at[0]),
        pltpu.make_async_copy(loud_v, loud, sem.at[1]),
    ]
    for copy in copies:
        copy.start()
    for copy in copies:
        copy.wait()


def shards(strain, fir_taps, templates):
    vmem_spec = pl.BlockSpec(memory_space=pltpu.VMEM)
    shapes = (
        jax.ShapeDtypeStruct((DET * 256, LANES), jnp.float32),
        jax.ShapeDtypeStruct((DET, BANK * LANES), jnp.float32),
    )
    hbm_spec = pl.BlockSpec(memory_space=pltpu.HBM)
    snr, loud = pl.pallas_call(
        kernel,
        out_shape=shapes,
        in_specs=[hbm_spec, hbm_spec, hbm_spec],
        out_specs=(vmem_spec, vmem_spec),
        scratch_shapes=[
            pltpu.VMEM((96 * 16, LANES), jnp.float32),
            pltpu.VMEM((TAPS // LANES, LANES), jnp.float32),
            pltpu.VMEM((2, 2, TLEN), jnp.bfloat16),
            pltpu.VMEM((2, 256, WOFF * 256), jnp.bfloat16),
            pltpu.VMEM((1024, COFF * 256), jnp.bfloat16),
            pltpu.VMEM(((WSTEP + WOFF - 1) * ROWS, 256), jnp.bfloat16),
            pltpu.VMEM(((WSTEP + WOFF - 1) * ROWS, 256), jnp.bfloat16),
            pltpu.VMEM((WSTEP * ROWS, 256), jnp.float32),
            pltpu.VMEM(((WSTEP + COFF - 1) * ROWS, 256), jnp.bfloat16),
            pltpu.VMEM((160 * 8, LANES), jnp.float32),
            pltpu.VMEM((BANK, 8, LANES), jnp.float32),
            pltpu.VMEM((DET, LANES), jnp.float32),
            pltpu.SemaphoreType.DMA((3,)),
            pltpu.SemaphoreType.DMA((4,)),
            pltpu.SemaphoreType.DMA((4,)),
            pltpu.SemaphoreType.DMA((2,)),
        ],
        compiler_params=pltpu.CompilerParams(
            collective_id=0, has_side_effects=True, vmem_limit_bytes=32 * 1024 * 1024
        ),
        name="matched_filter",
    )(*[pltpu.with_memory_space_constraint(v, pltpu.HBM) for v in (strain, fir_taps.reshape(TAPS // LANES, LANES), templates)])
    snr, loud = pl.pallas_call(
        place,
        out_shape=shapes,
        in_specs=[vmem_spec, vmem_spec],
        out_specs=(hbm_spec, hbm_spec),
        scratch_shapes=[pltpu.SemaphoreType.DMA((2,))],
        compiler_params=pltpu.CompilerParams(vmem_limit_bytes=1024 * 1024),
        name="place",
    )(snr, loud)
    snr = snr.reshape(DET, 128, 2, LANES).transpose(0, 2, 1, 3).reshape(DET, 2, 128 * LANES)
    return snr, loud


def solution(mesh):
    in_specs = (P(None, "tm", "bank"), P(), P("bank", None, None))
    out_specs = (P(None, "bank", "tm"), P(None, "tm"))
    return jax.shard_map(shards, mesh=mesh, in_specs=in_specs, out_specs=out_specs, check_vma=False)
```

```python
import jax
import jax.numpy as jnp
from jax import lax
from jax.experimental import pallas as pl
from jax.experimental.pallas import tpu as pltpu
from jax.sharding import PartitionSpec as P

MESH = pl.DeviceIdType.MESH
LANES = 128
DET = 3
NY, NZ, NX, NT = 8, 8, 2, 4
BANK = NY * NZ * NX
TAPS = 4096
TLEN = 2048
WSTEP = 5
WOFF = 17
COFF = 9
ROWS = 16 * DET


def far_first(i):
    half = (i + 1) // 2
    odd = i % 2
    return 4 + half - 2 * half * odd


def kernel(
    strain, taps, tmpl, snr, loud,
    gath, tap_v, tmpl_v, wtab, ctab, xh, xl, acc, cwin, sbuf, rbuf, res,
    in_sem, send_sem, recv_sem, halo_sem,
):
    b = lax.axis_index("bank")
    m = lax.axis_index("tm")
    y, z, x = b // 16, (b // 2) % 8, b % 2
    up, down = (m + 1) % NT, (m + NT - 1) % NT
    pairs = gath.reshape(96, 2, 8, LANES)

    def bank_of(yy, zz, xx):
        return yy * 16 + zz * 2 + xx

    barrier = pltpu.get_barrier_semaphore()

    def greet(dev):
        pl.semaphore_signal(barrier, inc=1, device_id=dev, device_id_type=MESH)

    for j in range(1, 8):
        jj = far_first(j - 1)
        greet((bank_of((y + jj) % NY, z, 1 - x), m))
        greet((bank_of(y, (z + jj) % NZ, 1 - x), m))
        greet((bank_of((y + jj) % NY, z, x), m))
        greet((bank_of(y, (z + jj) % NZ, x), m))
    greet((bank_of(y, z, 1 - x), m))
    for j in range(NZ):
        greet((bank_of(y, j, x), up))
        greet((bank_of(y, j, x), down))
    for yy in (0, 1):
        greet((bank_of(yy, z, x), up))
        greet((bank_of(6 + yy, z, x), down))

    own_row = pairs.at[12 + 8 * y + z, x, pl.ds(0, DET), :]
    load_own = pltpu.make_async_copy(strain.at[:, 0, :], own_row, in_sem.at[0])
    load_taps = pltpu.make_async_copy(taps, tap_v, in_sem.at[1])
    load_tmpl = pltpu.make_async_copy(tmpl, tmpl_v, in_sem.at[2])
    load_own.start()
    load_taps.start()
    load_tmpl.start()
    load_own.wait()
    load_taps.wait()
    load_tmpl.wait()

    row_id = lax.broadcasted_iota(jnp.int32, (LANES, LANES), 0)
    lane_id = lax.broadcasted_iota(jnp.int32, (LANES, LANES), 1)
    keep = lane_id >= row_id
    zero = jnp.zeros((LANES, LANES), jnp.float32)
    zero_b = jnp.zeros((LANES, LANES), jnp.bfloat16)

    def skew(row):
        wide = jnp.broadcast_to(row, (LANES, LANES))
        return pltpu.roll(wide, 0, 1, stride=1, stride_axis=0)

    def tap_table():
        last = zero
        for c in range(TAPS // LANES + 1):
            if c < TAPS // LANES:
                now = skew(tap_v[pl.ds(c, 1), :])
            else:
                now = zero
            tile = jnp.where(keep, now, last)
            last = now
            hi = tile.astype(jnp.bfloat16)
            lo = (tile - hi.astype(jnp.float32)).astype(jnp.bfloat16)
            for part, val in enumerate((hi, lo)):
                wtab[part, 0:128, c * 128:(c + 1) * 128] = val
                wtab[part, 128:256, (c + 1) * 128:(c + 2) * 128] = val
        for part in range(2):
            wtab[part, 0:128, 33 * 128:34 * 128] = zero_b
            wtab[part, 128:256, 0:128] = zero_b

    def tmpl_table(f):
        last = zero
        rows = tmpl_v[f // 2].astype(jnp.float32)
        top, low = slice(f * 256, f * 256 + 128), slice(f * 256 + 128, f * 256 + 256)
        for c in range(TLEN // LANES + 1):
            if c < TLEN // LANES:
                now = skew(rows[f % 2:f % 2 + 1, c * 128:(c + 1) * 128])
            else:
                now = zero
            tile = jnp.where(keep, now, last).astype(jnp.bfloat16)
            last = now
            ctab[top, c * 128:(c + 1) * 128] = tile
            ctab[low, (c + 1) * 128:(c + 2) * 128] = tile
        ctab[top, 17 * 128:18 * 128] = zero_b
        ctab[low, 0:128] = zero_b

    tap_table()
    tmpl_table(0)
    tmpl_table(1)
    edge = jnp.where((y <= 1) | (y >= 6), NY, 0)
    pl.semaphore_wait(barrier, 29 + 2 * NZ + edge)

    def send_a(p):
        pltpu.make_async_remote_copy(
            src_ref=own_row, dst_ref=own_row, send_sem=send_sem.at[0], recv_sem=recv_sem.at[0],
            device_id=(p, m), device_id_type=MESH,
        ).start()

    for j in range(15):
        jj, dx = far_first(j // 2), 1 - j % 2
        send_a(jnp.where(
            x == 0, bank_of((y + jj) % NY, z, (x + dx) % NX), bank_of(y, (z + jj) % NZ, (x + dx) % NX)
        ))
    tmpl_table(2)
    tmpl_table(3)
    inv = []
    for k in range(2):
        wide = tmpl_v[k].astype(jnp.float32)
        energy = jnp.sum(wide * wide, keepdims=True) / (2.0 * TLEN) + 1e-6
        inv.append(1.0 / (TLEN * energy))

    got = pairs.at[pl.ds(0, 15), 0, pl.ds(0, DET), :]
    pltpu.make_async_copy(got, got, recv_sem.at[0]).wait()

    def send_b(src, dst, sem, p, to):
        pltpu.make_async_remote_copy(
            src_ref=src, dst_ref=dst, send_sem=sem, recv_sem=recv_sem.at[1],
            device_id=(p, to), device_id_type=MESH,
        ).start()

    eights = gath.reshape(12, 8, 2, 8, LANES)
    at_q, at_r = (12 + z) // 8, (z + 4) % 8
    yline = eights.at[pl.ds(at_q, 8), at_r, 0, pl.ds(0, DET), :]
    zline = pairs.at[pl.ds(12 + 8 * y, 8), 1, pl.ds(0, DET), :]
    def margin_y(cond, src_at, dst_at, count, to):
        @pl.when(cond)
        def _():
            for j in range(NY):
                send_b(
                    pairs.at[pl.ds(src_at, count), 1, pl.ds(0, DET), :],
                    pairs.at[pl.ds(dst_at, count), 1, pl.ds(0, DET), :],
                    halo_sem.at[0], bank_of((y + far_first(j)) % NY, z, x), to,
                )

    margin_y(y == 0, 12, 76, 8, down)
    margin_y(y == 1, 20, 84, 4, down)
    margin_y(y == 6, 64, 0, 4, up)
    margin_y(y == 7, 68, 4, 8, up)

    def margin_z(cond, low, high):
        @pl.when(cond)
        def _():
            for j in range(NZ):
                p = bank_of(y, (z + far_first(j)) % NZ, x)
                send_b(
                    eights.at[pl.ds(at_q, low), at_r, 0, pl.ds(0, DET), :],
                    eights.at[pl.ds(at_q + 8, low), at_r, 0, pl.ds(0, DET), :],
                    halo_sem.at[1], p, down,
                )
                send_b(
                    eights.at[pl.ds(8, high), at_r, 0, pl.ds(0, DET), :],
                    eights.at[pl.ds(0, high), at_r, 0, pl.ds(0, DET), :],
                    halo_sem.at[1], p, up,
                )

    margin_z(z < 4, 2, 1)
    margin_z(z >= 4, 1, 2)

    for j in range(7):
        send_b(zline, zline, send_sem.at[1], bank_of((y + far_first(j)) % NY, z, x), m)
    for j in range(7):
        send_b(yline, yline, send_sem.at[1], bank_of(y, (z + far_first(j)) % NZ, x), m)

    got = pairs.at[pl.ds(0, 80), :, pl.ds(0, DET), :]
    pltpu.make_async_copy(got, got, recv_sem.at[1]).wait()

    nt = (((1,), (1,)), ((), ()))

    @pl.when(b >= 0)
    def _():
        for a in range(WSTEP + WOFF - 1):
            for d in range(DET):
                rows = slice(a * ROWS + d * 16, a * ROWS + d * 16 + 16)
                for h in range(2):
                    val = gath[pl.ds(8 * (2 * a + h) + d, 16, stride=16 * WSTEP), :]
                    hi = val.astype(jnp.bfloat16)
                    lo = (val - hi.astype(jnp.float32)).astype(jnp.bfloat16)
                    xh[rows, h * 128:(h + 1) * 128] = hi
                    xl[rows, h * 128:(h + 1) * 128] = lo
        hi_all = jnp.concatenate([xh[o * ROWS:(o + WSTEP) * ROWS, :] for o in range(WOFF)], axis=1)
        lo_all = jnp.concatenate([xl[o * ROWS:(o + WSTEP) * ROWS, :] for o in range(WOFF)], axis=1)
        both = lax.dot_general(
            jnp.concatenate([hi_all, lo_all], axis=0), wtab[0], nt, preferred_element_type=jnp.float32
        )
        acc[...] = both[:WSTEP * ROWS] + both[WSTEP * ROWS:] + lax.dot_general(
            hi_all, wtab[1], nt, preferred_element_type=jnp.float32
        )

    n_out = WSTEP * ROWS
    out = acc[...]
    n_more = (COFF - 1 - WSTEP) * ROWS
    cwin[0:n_out, :] = out.astype(jnp.bfloat16)
    cwin[n_out:2 * n_out, :] = pltpu.roll(out, n_out - 1, 0).astype(jnp.bfloat16)
    cwin[2 * n_out:2 * n_out + n_more, :] = pltpu.roll(out, n_out - 2, 0)[:n_more].astype(jnp.bfloat16)
    wins = jnp.concatenate([cwin[o * ROWS:o * ROWS + n_out, :] for o in range(COFF)], axis=1)
    corr = lax.dot_general(wins, ctab[...], nt, preferred_element_type=jnp.float32)
    power = []
    for k in range(2):
        c0 = corr[:, k * 512:k * 512 + 256]
        c1 = corr[:, k * 512 + 256:k * 512 + 512]
        power.append((c0 * c0 + c1 * c1) * inv[k])
    best = jnp.maximum(power[0], power[1])
    for a in range(WSTEP):
        for d in range(DET):
            rows = slice(a * ROWS + d * 16, a * ROWS + d * 16 + 16)
            for h in range(2):
                sbuf[pl.ds(8 * (2 * a + h) + d, 16, stride=16 * WSTEP), :] = best[rows, h * 128:(h + 1) * 128]

    send3 = sbuf.reshape(160, 8, LANES)

    ys = [((y + j) % NY) * 16 for j in range(NY)]
    zs = [((z + j) % NZ) * 2 for j in range(NZ)]
    xs = [x, 1 - x]
    steps = sorted(
        ((2 * jx + min(jy, NY - jy) + min(jz, NZ - jz), jx, jy, jz)
         for jx in range(NX) for jy in range(NY) for jz in range(NZ)), reverse=True
    )[:BANK - 1]

    def to_all(make):
        for n, (hops, jx, jy, jz) in enumerate(steps):
            make(ys[jy] + zs[jz] + xs[jx]).start()

    to_all(lambda p: pltpu.make_async_remote_copy(
        src_ref=send3.at[p, pl.ds(0, DET), :], dst_ref=rbuf.at[b, pl.ds(0, DET), :],
        send_sem=send_sem.at[2], recv_sem=recv_sem.at[2],
        device_id=(p, m), device_id_type=MESH,
    ))
    for a in range(WSTEP):
        count = (63 - a) // WSTEP + 1
        for d in range(DET):
            rows = slice(a * ROWS + d * 16, a * ROWS + d * 16 + count)
            for h in range(2):
                for k in range(2):
                    snr[pl.ds(d * 256 + 2 * (2 * a + h) + k, count, stride=4 * WSTEP), :] = (
                        power[k][rows, h * 128:(h + 1) * 128]
                    )
    own = send3[b, 0:DET, :]
    got = rbuf.at[pl.ds(0, BANK - 1), pl.ds(0, DET), :]
    pltpu.make_async_copy(got, got, recv_sem.at[2]).wait()
    rbuf[b, 0:DET, :] = own
    top = jnp.max(rbuf[:, 0:DET, :], axis=0)
    res[...] = top
    mine = pl.ds(pl.multiple_of(b * 128, 128), 128)

    def spread(p):
        return pltpu.make_async_remote_copy(
            src_ref=res, dst_ref=loud.at[:, mine],
            send_sem=send_sem.at[3], recv_sem=recv_sem.at[3],
            device_id=(p, m), device_id_type=MESH,
        )

    planes = sorted(
        ((2 * jx + min(jy, NY - jy), jx, jy) for jx in range(NX) for jy in range(NY)), reverse=True
    )
    for zz in range(NZ):
        for hops, jx, jy in planes:
            copy = spread(ys[jy] + 2 * zz + xs[jx])
            if hops:
                copy.start()
            else:
                pl.when(z != zz)(copy.start)
    loud[:, mine] = top
    got = rbuf.at[pl.ds(0, BANK - 1), pl.ds(0, DET), :]
    pltpu.make_async_copy(got, got, recv_sem.at[3]).wait()
    sent = pairs.at[pl.ds(0, 15), 0, pl.ds(0, DET), :]
    pltpu.make_async_copy(sent, sent, send_sem.at[0]).wait()
    sent = pairs.at[pl.ds(0, 56), :, pl.ds(0, DET), :]
    pltpu.make_async_copy(sent, sent, send_sem.at[1]).wait()
    part = pairs.at[pl.ds(0, 12), :, pl.ds(0, DET), :]
    pltpu.make_async_copy(part, part, halo_sem.at[1]).wait()

    @pl.when((y == 0) | (y == 7))
    def _():
        part = pairs.at[pl.ds(0, 32), :, pl.ds(0, DET), :]
        pltpu.make_async_copy(part, part, halo_sem.at[0]).wait()

    @pl.when((y == 1) | (y == 6))
    def _():
        part = pairs.at[pl.ds(0, 16), :, pl.ds(0, DET), :]
        pltpu.make_async_copy(part, part, halo_sem.at[0]).wait()

    sent = rbuf.at[pl.ds(0, BANK - 1), pl.ds(0, DET), :]
    pltpu.make_async_copy(sent, sent, send_sem.at[2]).wait()
    pltpu.make_async_copy(sent, sent, send_sem.at[3]).wait()


def place(snr_v, loud_v, snr, loud, sem):
    copies = [
        pltpu.make_async_copy(snr_v, snr, sem.at[0]),
        pltpu.make_async_copy(loud_v, loud, sem.at[1]),
    ]
    for copy in copies:
        copy.start()
    for copy in copies:
        copy.wait()


def shards(strain, fir_taps, templates):
    vmem_spec = pl.BlockSpec(memory_space=pltpu.VMEM)
    shapes = (
        jax.ShapeDtypeStruct((DET * 256, LANES), jnp.float32),
        jax.ShapeDtypeStruct((DET, BANK * LANES), jnp.float32),
    )
    hbm_spec = pl.BlockSpec(memory_space=pltpu.HBM)
    snr, loud = pl.pallas_call(
        kernel,
        out_shape=shapes,
        in_specs=[hbm_spec, hbm_spec, hbm_spec],
        out_specs=(vmem_spec, vmem_spec),
        scratch_shapes=[
            pltpu.VMEM((96 * 16, LANES), jnp.float32),
            pltpu.VMEM((TAPS // LANES, LANES), jnp.float32),
            pltpu.VMEM((2, 2, TLEN), jnp.bfloat16),
            pltpu.VMEM((2, 256, WOFF * 256), jnp.bfloat16),
            pltpu.VMEM((1024, COFF * 256), jnp.bfloat16),
            pltpu.VMEM(((WSTEP + WOFF - 1) * ROWS, 256), jnp.bfloat16),
            pltpu.VMEM(((WSTEP + WOFF - 1) * ROWS, 256), jnp.bfloat16),
            pltpu.VMEM((WSTEP * ROWS, 256), jnp.float32),
            pltpu.VMEM(((WSTEP + COFF - 1) * ROWS, 256), jnp.bfloat16),
            pltpu.VMEM((160 * 8, LANES), jnp.float32),
            pltpu.VMEM((BANK, 8, LANES), jnp.float32),
            pltpu.VMEM((DET, LANES), jnp.float32),
            pltpu.SemaphoreType.DMA((3,)),
            pltpu.SemaphoreType.DMA((4,)),
            pltpu.SemaphoreType.DMA((4,)),
            pltpu.SemaphoreType.DMA((2,)),
        ],
        compiler_params=pltpu.CompilerParams(
            collective_id=0, has_side_effects=True, vmem_limit_bytes=32 * 1024 * 1024
        ),
        name="matched_filter",
    )(*[pltpu.with_memory_space_constraint(v, pltpu.HBM) for v in (strain, fir_taps.reshape(TAPS // LANES, LANES), templates)])
    snr, loud = pl.pallas_call(
        place,
        out_shape=shapes,
        in_specs=[vmem_spec, vmem_spec],
        out_specs=(hbm_spec, hbm_spec),
        scratch_shapes=[pltpu.SemaphoreType.DMA((2,))],
        compiler_params=pltpu.CompilerParams(vmem_limit_bytes=1024 * 1024),
        name="place",
    )(snr, loud)
    snr = snr.reshape(DET, 128, 2, LANES).transpose(0, 2, 1, 3).reshape(DET, 2, 128 * LANES)
    return snr, loud


def solution(mesh):
    in_specs = (P(None, "tm", "bank"), P(), P("bank", None, None))
    out_specs = (P(None, "bank", "tm"), P(None, "tm"))
    return jax.shard_map(shards, mesh=mesh, in_specs=in_specs, out_specs=out_specs, check_vma=False)
```

```python
import jax
import jax.numpy as jnp
from jax import lax
from jax.experimental import pallas as pl
from jax.experimental.pallas import tpu as pltpu
from jax.sharding import PartitionSpec as P

MESH = pl.DeviceIdType.MESH
LANES = 128
DET = 3
NY, NZ, NX, NT = 8, 8, 2, 4
BANK = NY * NZ * NX
TAPS = 4096
TLEN = 2048
WSTEP = 5
WOFF = 17
COFF = 9
ROWS = 16 * DET
SNR_ROWS = 832


def far_first(i):
    half = (i + 1) // 2
    odd = i % 2
    return 4 + half - 2 * half * odd


def kernel(
    strain, taps, tmpl, snr, loud,
    gath, tap_v, tmpl_v, wtab, ctab, xh, xl, acc, cwin, sbuf, rbuf, res,
    in_sem, send_sem, recv_sem, halo_sem,
):
    b = lax.axis_index("bank")
    m = lax.axis_index("tm")
    y, z, x = b // 16, (b // 2) % 8, b % 2
    up, down = (m + 1) % NT, (m + NT - 1) % NT
    pairs = gath.reshape(96, 2, 8, LANES)

    def bank_of(yy, zz, xx):
        return yy * 16 + zz * 2 + xx

    barrier = pltpu.get_barrier_semaphore()

    def greet(dev):
        pl.semaphore_signal(barrier, inc=1, device_id=dev, device_id_type=MESH)

    for j in range(1, 8):
        jj = far_first(j - 1)
        greet((bank_of((y + jj) % NY, z, 1 - x), m))
        greet((bank_of(y, (z + jj) % NZ, 1 - x), m))
        greet((bank_of((y + jj) % NY, z, x), m))
        greet((bank_of(y, (z + jj) % NZ, x), m))
    greet((bank_of(y, z, 1 - x), m))
    for j in range(NZ):
        greet((bank_of(y, j, x), up))
        greet((bank_of(y, j, x), down))
    for yy in (0, 1):
        greet((bank_of(yy, z, x), up))
        greet((bank_of(6 + yy, z, x), down))

    own_row = pairs.at[12 + 8 * y + z, x, pl.ds(0, DET), :]
    load_own = pltpu.make_async_copy(strain.at[:, 0, :], own_row, in_sem.at[0])
    load_taps = pltpu.make_async_copy(taps, tap_v, in_sem.at[1])
    load_tmpl = pltpu.make_async_copy(tmpl, tmpl_v.at[pl.ds(0, 2)], in_sem.at[2])
    load_own.start()
    load_taps.start()
    load_tmpl.start()
    load_own.wait()
    load_taps.wait()
    load_tmpl.wait()

    row_id = lax.broadcasted_iota(jnp.int32, (LANES, LANES), 0)
    lane_id = lax.broadcasted_iota(jnp.int32, (LANES, LANES), 1)
    keep = lane_id >= row_id
    zero = jnp.zeros((LANES, LANES), jnp.float32)
    zero_b = jnp.zeros((LANES, LANES), jnp.bfloat16)

    def skew(row):
        wide = jnp.broadcast_to(row, (LANES, LANES))
        return pltpu.roll(wide, 0, 1, stride=1, stride_axis=0)

    def tap_table():
        last = zero
        for c in range(TAPS // LANES + 1):
            if c < TAPS // LANES:
                now = skew(tap_v[pl.ds(c, 1), :])
            else:
                now = zero
            tile = jnp.where(keep, now, last)
            last = now
            hi = tile.astype(jnp.bfloat16)
            lo = (tile - hi.astype(jnp.float32)).astype(jnp.bfloat16)
            for part, val in enumerate((hi, lo)):
                wtab[part, 0:128, c * 128:(c + 1) * 128] = val
                wtab[part, 128:256, (c + 1) * 128:(c + 2) * 128] = val
        for part in range(2):
            wtab[part, 0:128, 33 * 128:34 * 128] = zero_b
            wtab[part, 128:256, 0:128] = zero_b

    def tmpl_table(f):
        last = zero
        rows = tmpl_v[f // 2].astype(jnp.float32)
        top, low = slice(f * 256, f * 256 + 128), slice(f * 256 + 128, f * 256 + 256)
        for c in range(TLEN // LANES + 1):
            if c < TLEN // LANES:
                now = skew(rows[f % 2:f % 2 + 1, c * 128:(c + 1) * 128])
            else:
                now = zero
            tile = jnp.where(keep, now, last).astype(jnp.bfloat16)
            last = now
            ctab[top, c * 128:(c + 1) * 128] = tile
            ctab[low, (c + 1) * 128:(c + 2) * 128] = tile
        ctab[top, 17 * 128:18 * 128] = zero_b
        ctab[low, 0:128] = zero_b

    tap_table()
    tmpl_table(0)
    tmpl_table(1)
    edge = jnp.where((y <= 1) | (y >= 6), NY, 0)
    pl.semaphore_wait(barrier, 29 + 2 * NZ + edge)

    def send_a(p):
        pltpu.make_async_remote_copy(
            src_ref=own_row, dst_ref=own_row, send_sem=send_sem.at[0], recv_sem=recv_sem.at[0],
            device_id=(p, m), device_id_type=MESH,
        ).start()

    for j in range(15):
        jj, dx = far_first(j // 2), 1 - j % 2
        send_a(jnp.where(
            x == 0, bank_of((y + jj) % NY, z, (x + dx) % NX), bank_of(y, (z + jj) % NZ, (x + dx) % NX)
        ))
    tmpl_table(2)
    tmpl_table(3)
    inv = []
    for k in range(2):
        wide = tmpl_v[k].astype(jnp.float32)
        energy = jnp.sum(wide * wide, keepdims=True) / (2.0 * TLEN) + 1e-6
        inv.append(1.0 / (TLEN * energy))

    got = pairs.at[pl.ds(0, 15), 0, pl.ds(0, DET), :]
    pltpu.make_async_copy(got, got, recv_sem.at[0]).wait()

    def send_b(src, dst, sem, p, to):
        pltpu.make_async_remote_copy(
            src_ref=src, dst_ref=dst, send_sem=sem, recv_sem=recv_sem.at[1],
            device_id=(p, to), device_id_type=MESH,
        ).start()

    eights = gath.reshape(12, 8, 2, 8, LANES)
    at_q, at_r = (12 + z) // 8, (z + 4) % 8
    yline = eights.at[pl.ds(at_q, 8), at_r, 0, pl.ds(0, DET), :]
    zline = pairs.at[pl.ds(12 + 8 * y, 8), 1, pl.ds(0, DET), :]
    def margin_y(cond, src_at, dst_at, count, to):
        @pl.when(cond)
        def _():
            for j in range(NY):
                send_b(
                    pairs.at[pl.ds(src_at, count), 1, pl.ds(0, DET), :],
                    pairs.at[pl.ds(dst_at, count), 1, pl.ds(0, DET), :],
                    halo_sem.at[0], bank_of((y + far_first(j)) % NY, z, x), to,
                )

    margin_y(y == 0, 12, 76, 8, down)
    margin_y(y == 1, 20, 84, 4, down)
    margin_y(y == 6, 64, 0, 4, up)
    margin_y(y == 7, 68, 4, 8, up)

    def margin_z(cond, low, high):
        @pl.when(cond)
        def _():
            for j in range(NZ):
                p = bank_of(y, (z + far_first(j)) % NZ, x)
                send_b(
                    eights.at[pl.ds(at_q, low), at_r, 0, pl.ds(0, DET), :],
                    eights.at[pl.ds(at_q + 8, low), at_r, 0, pl.ds(0, DET), :],
                    halo_sem.at[1], p, down,
                )
                send_b(
                    eights.at[pl.ds(8, high), at_r, 0, pl.ds(0, DET), :],
                    eights.at[pl.ds(0, high), at_r, 0, pl.ds(0, DET), :],
                    halo_sem.at[1], p, up,
                )

    margin_z(z < 4, 2, 1)
    margin_z(z >= 4, 1, 2)

    for j in range(7):
        send_b(zline, zline, send_sem.at[1], bank_of((y + far_first(j)) % NY, z, x), m)
    for j in range(7):
        send_b(yline, yline, send_sem.at[1], bank_of(y, (z + far_first(j)) % NZ, x), m)

    got = pairs.at[pl.ds(0, 80), :, pl.ds(0, DET), :]
    pltpu.make_async_copy(got, got, recv_sem.at[1]).wait()

    nt = (((1,), (1,)), ((), ()))

    @pl.when(b >= 0)
    def _():
        for a in range(WSTEP + WOFF - 1):
            for d in range(DET):
                rows = slice(a * ROWS + d * 16, a * ROWS + d * 16 + 16)
                for h in range(2):
                    val = gath[pl.ds(8 * (2 * a + h) + d, 16, stride=16 * WSTEP), :]
                    hi = val.astype(jnp.bfloat16)
                    lo = (val - hi.astype(jnp.float32)).astype(jnp.bfloat16)
                    xh[rows, h * 128:(h + 1) * 128] = hi
                    xl[rows, h * 128:(h + 1) * 128] = lo
        hi_all = jnp.concatenate([xh[o * ROWS:(o + WSTEP) * ROWS, :] for o in range(WOFF)], axis=1)
        lo_all = jnp.concatenate([xl[o * ROWS:(o + WSTEP) * ROWS, :] for o in range(WOFF)], axis=1)
        both = lax.dot_general(
            jnp.concatenate([hi_all, lo_all], axis=0), wtab[0], nt, preferred_element_type=jnp.float32
        )
        acc[...] = both[:WSTEP * ROWS] + both[WSTEP * ROWS:] + lax.dot_general(
            hi_all, wtab[1], nt, preferred_element_type=jnp.float32
        )

    n_out = WSTEP * ROWS
    out = acc[...]
    n_more = (COFF - 1 - WSTEP) * ROWS
    cwin[0:n_out, :] = out.astype(jnp.bfloat16)
    cwin[n_out:2 * n_out, :] = pltpu.roll(out, n_out - 1, 0).astype(jnp.bfloat16)
    cwin[2 * n_out:2 * n_out + n_more, :] = pltpu.roll(out, n_out - 2, 0)[:n_more].astype(jnp.bfloat16)
    wins = jnp.concatenate([cwin[o * ROWS:o * ROWS + n_out, :] for o in range(COFF)], axis=1)
    corr = lax.dot_general(wins, ctab[...], nt, preferred_element_type=jnp.float32)
    power = []
    for k in range(2):
        c0 = corr[:, k * 512:k * 512 + 256]
        c1 = corr[:, k * 512 + 256:k * 512 + 512]
        power.append((c0 * c0 + c1 * c1) * inv[k])
    best = jnp.maximum(power[0], power[1])
    for a in range(WSTEP):
        for d in range(DET):
            rows = slice(a * ROWS + d * 16, a * ROWS + d * 16 + 16)
            for h in range(2):
                sbuf[pl.ds(8 * (2 * a + h) + d, 16, stride=16 * WSTEP), :] = best[rows, h * 128:(h + 1) * 128]

    send3 = sbuf.reshape(160, 8, LANES)

    ys = [((y + j) % NY) * 16 for j in range(NY)]
    zs = [((z + j) % NZ) * 2 for j in range(NZ)]
    xs = [x, 1 - x]
    steps = sorted(
        ((2 * jx + min(jy, NY - jy) + min(jz, NZ - jz), jx, jy, jz)
         for jx in range(NX) for jy in range(NY) for jz in range(NZ)), reverse=True
    )[:BANK - 1]

    def to_all(make):
        for n, (hops, jx, jy, jz) in enumerate(steps):
            make(ys[jy] + zs[jz] + xs[jx]).start()

    to_all(lambda p: pltpu.make_async_remote_copy(
        src_ref=send3.at[p, pl.ds(0, DET), :], dst_ref=rbuf.at[b, pl.ds(0, DET), :],
        send_sem=send_sem.at[2], recv_sem=recv_sem.at[2],
        device_id=(p, m), device_id_type=MESH,
    ))
    for a in range(WSTEP):
        count = (63 - a) // WSTEP + 1
        for d in range(DET):
            rows = slice(a * ROWS + d * 16, a * ROWS + d * 16 + count)
            for h in range(2):
                for k in range(2):
                    snr[pl.ds(d * 256 + 2 * (2 * a + h) + k, count, stride=4 * WSTEP), :] = (
                        power[k][rows, h * 128:(h + 1) * 128]
                    )
    own = send3[b, 0:DET, :]
    got = rbuf.at[pl.ds(0, BANK - 1), pl.ds(0, DET), :]
    pltpu.make_async_copy(got, got, recv_sem.at[2]).wait()
    rbuf[b, 0:DET, :] = own
    top = jnp.max(rbuf[:, 0:DET, :], axis=0)
    res[0:DET, :] = top
    final = res.at[pl.ds(0, DET), :]
    mine = pl.ds(pl.multiple_of(b * 128, 128), 128)

    def spread(p):
        return pltpu.make_async_remote_copy(
            src_ref=final, dst_ref=loud.at[:, mine],
            send_sem=send_sem.at[3], recv_sem=recv_sem.at[3],
            device_id=(p, m), device_id_type=MESH,
        )

    planes = sorted(
        ((2 * jx + min(jy, NY - jy), jx, jy) for jx in range(NX) for jy in range(NY)), reverse=True
    )
    for zz in range(NZ):
        for hops, jx, jy in planes:
            copy = spread(ys[jy] + 2 * zz + xs[jx])
            if hops:
                copy.start()
            else:
                pl.when(z != zz)(copy.start)
    keep_own = pltpu.make_async_copy(final, loud.at[:, mine], in_sem.at[1])
    keep_own.start()
    keep_own.wait()
    got = rbuf.at[pl.ds(0, BANK - 1), pl.ds(0, DET), :]
    pltpu.make_async_copy(got, got, recv_sem.at[3]).wait()
    sent = pairs.at[pl.ds(0, 15), 0, pl.ds(0, DET), :]
    pltpu.make_async_copy(sent, sent, send_sem.at[0]).wait()
    sent = pairs.at[pl.ds(0, 56), :, pl.ds(0, DET), :]
    pltpu.make_async_copy(sent, sent, send_sem.at[1]).wait()
    part = pairs.at[pl.ds(0, 12), :, pl.ds(0, DET), :]
    pltpu.make_async_copy(part, part, halo_sem.at[1]).wait()

    @pl.when((y == 0) | (y == 7))
    def _():
        part = pairs.at[pl.ds(0, 32), :, pl.ds(0, DET), :]
        pltpu.make_async_copy(part, part, halo_sem.at[0]).wait()

    @pl.when((y == 1) | (y == 6))
    def _():
        part = pairs.at[pl.ds(0, 16), :, pl.ds(0, DET), :]
        pltpu.make_async_copy(part, part, halo_sem.at[0]).wait()

    sent = rbuf.at[pl.ds(0, BANK - 1), pl.ds(0, DET), :]
    pltpu.make_async_copy(sent, sent, send_sem.at[2]).wait()
    pltpu.make_async_copy(sent, sent, send_sem.at[3]).wait()


def place(snr_v, loud_v, snr, loud, sem):
    copies = [
        pltpu.make_async_copy(snr_v.at[pl.ds(0, DET * 256), :], snr, sem.at[0]),
        pltpu.make_async_copy(loud_v, loud, sem.at[1]),
    ]
    for copy in copies:
        copy.start()
    for copy in copies:
        copy.wait()


def shards(strain, fir_taps, templates):
    vmem_spec = pl.BlockSpec(memory_space=pltpu.VMEM)
    shapes = (
        jax.ShapeDtypeStruct((DET * 256, LANES), jnp.float32),
        jax.ShapeDtypeStruct((DET, BANK * LANES), jnp.float32),
    )
    hbm_spec = pl.BlockSpec(memory_space=pltpu.HBM)
    snr, loud = pl.pallas_call(
        kernel,
        out_shape=(jax.ShapeDtypeStruct((SNR_ROWS, LANES), jnp.float32), shapes[1]),
        in_specs=[hbm_spec, hbm_spec, hbm_spec],
        out_specs=(vmem_spec, vmem_spec),
        scratch_shapes=[
            pltpu.VMEM((96 * 16, LANES), jnp.float32),
            pltpu.VMEM((TAPS // LANES, LANES), jnp.float32),
            pltpu.VMEM((4, 2, TLEN), jnp.bfloat16),
            pltpu.VMEM((2, 256, WOFF * 256), jnp.bfloat16),
            pltpu.VMEM((1024, COFF * 256), jnp.bfloat16),
            pltpu.VMEM(((WSTEP + WOFF - 1) * ROWS, 256), jnp.bfloat16),
            pltpu.VMEM(((WSTEP + WOFF - 1) * ROWS, 256), jnp.bfloat16),
            pltpu.VMEM((WSTEP * ROWS, 256), jnp.float32),
            pltpu.VMEM(((WSTEP + COFF - 1) * ROWS, 256), jnp.bfloat16),
            pltpu.VMEM((160 * 8, LANES), jnp.float32),
            pltpu.VMEM((BANK, 8, LANES), jnp.float32),
            pltpu.VMEM((8, LANES), jnp.float32),
            pltpu.SemaphoreType.DMA((3,)),
            pltpu.SemaphoreType.DMA((4,)),
            pltpu.SemaphoreType.DMA((4,)),
            pltpu.SemaphoreType.DMA((2,)),
        ],
        compiler_params=pltpu.CompilerParams(
            collective_id=0, has_side_effects=True, vmem_limit_bytes=32 * 1024 * 1024
        ),
        name="matched_filter",
    )(*[pltpu.with_memory_space_constraint(v, pltpu.HBM) for v in (strain, fir_taps.reshape(TAPS // LANES, LANES), templates)])
    snr, loud = pl.pallas_call(
        place,
        out_shape=shapes,
        in_specs=[vmem_spec, vmem_spec],
        out_specs=(hbm_spec, hbm_spec),
        scratch_shapes=[pltpu.SemaphoreType.DMA((2,))],
        compiler_params=pltpu.CompilerParams(vmem_limit_bytes=1024 * 1024),
        name="place",
    )(snr, loud)
    snr = snr.reshape(DET, 128, 2, LANES).transpose(0, 2, 1, 3).reshape(DET, 2, 128 * LANES)
    return snr, loud


def solution(mesh):
    in_specs = (P(None, "tm", "bank"), P(), P("bank", None, None))
    out_specs = (P(None, "bank", "tm"), P(None, "tm"))
    return jax.shard_map(shards, mesh=mesh, in_specs=in_specs, out_specs=out_specs, check_vma=False)
```
